32 devices in a mesh: pole: 2 (over x), row: 8 (over z, y), col: 2 (over core).
Axes of the slice: x: 2, y: 2, z: 4, core: 2. Of those that a mesh axis runs over, the one named last changes fastest.
Arguments:
- ancestor_inverse: float32 [24576, 12288], P(('pole', 'row'), 'col'), parts along dimension 0, may hold values from -0.0546875 to 0.0546875
- parent_panel: float32 [24576, 256], P(('pole', 'row'), 'col'), parts along dimension 0, may hold values from -0.0546875 to 0.0546875
- child_panel: float32 [24576, 256], P(('pole', 'row'), 'col'), parts along dimension 0, may hold values from -0.0546875 to 0.0546875
- child_link: float32 [4, 128, 128], P(('pole', 'col')), parts along dimension 0, may hold values from -0.5 to 0.5
- parent_pivot_inv: float32 [4, 128, 128], P(('pole', 'col')), parts along dimension 0, may hold values from -6 to 6
- child_pivot_inv: float32 [4, 128, 128], P(('pole', 'col')), parts along dimension 0, may hold values from -6 to 6
- parent_blocks: int32 [4, 96], P('pole'), parts along dimension 0, may hold values 0 or 1
- child_blocks: int32 [4, 96], P('pole'), parts along dimension 0, may hold values 0 or 1
- tree: int32 [4], P('pole'), parts along dimension 0, may hold values from 0 to 1, as said below
Outputs:
- parent_column: float32 [24576, 256], P(('pole', 'row'), 'col'), parts along dimension 0
- parent_diag: float32 [4, 128, 128], P(('pole', 'col')), parts along dimension 0
- child_column: float32 [24576, 256], P(('pole', 'row'), 'col'), parts along dimension 0
- child_cross: float32 [4, 128, 128], P(('pole', 'col')), parts along dimension 0
- child_diag: float32 [4, 128, 128], P(('pole', 'col')), parts along dimension 0
The draws below stay inside these ranges and needn't reach their ends.
There are 2 independent parts, one for each index of `pole`. The reference program is written for one: setup_inputs(seed, part) draws one part's arguments, and reference() takes and returns one part's arrays. A program takes and returns all parts, laid end to end along the dimension named above; each array names one. Nothing has to cross between parts.
Inputs may be any that keep to these rules, and one draw needn't show every extreme that they name: `tree`: each child's parent among the 2 parent supernodes; every parent has the same number of children.
All inputs are finite; a program needn't handle non-finite values.
Results may differ from the reference program's by a relative error of at most 0.000071.
Values sent between devices are 32-bit elements; how exact they have to be, the bound alone decides.
A program may use at most 192 MiB of HBM per device.

```python
import jax
import jax.numpy as jnp
from jax import lax

W = 128
NB = 96
NS = 12288
NP = 2
NC = 2


def draw_tree(key, part):
    key = jax.random.fold_in(key, 7)
    order = jax.random.permutation(key, NC)
    return (order % NP).astype(jnp.int32)


def plant(array, stream_key, low, high):
    longest = array.shape.index(max(array.shape))
    spots = []
    for shift in (0, 1):
        where = [jax.random.randint(jax.random.fold_in(stream_key, axis), (), 0, length) for axis, length in enumerate(array.shape)]
        where[longest] = (where[longest] + shift) % array.shape[longest]
        spots.append(tuple(where))
    return array.at[spots[0]].set(low).at[spots[1]].set(high)


def steps_of(own_key, shape, cuts, least, top_value):
    factor_of, own = 1.0, jax.random.fold_in(own_key, 6)
    for dim, shards_of in cuts:
        heights = jnp.exp(jax.random.uniform(jax.random.fold_in(own, dim), (shards_of,), jnp.float32, least / len(cuts), top_value / len(cuts)))
        factor_of = factor_of * jnp.repeat(heights, shape[dim] // shards_of).reshape([-1 if axis == dim else 1 for axis in range(len(shape))])
    return factor_of


def scatter_about(own_key, dims, scale, limit, shards=(), kind=jnp.bfloat16):
    drawn = jax.random.normal(own_key, dims, jnp.float32) * scale
    if len(shards) > 0:
        drawn = steps_of(own_key, dims, shards, -0.22, 0.18) * drawn
    return jnp.clip(drawn, min=-limit, max=limit).astype(kind)


def setup_inputs(seed: int = 0, part: int = 0) -> dict:
    seeds = jax.random.split(jax.random.key(seed), 10)
    part_keys = jax.random.split(jax.random.fold_in(seeds[9], part), 10)
    ancestor_inverse = scatter_about(part_keys[0], (NS, NS), NS ** -0.5, 0.0546875, ((0, 8), (1, 2)), jnp.float32)
    parent_panel = scatter_about(part_keys[1], (NS, NP * W), NS ** -0.5, 0.0546875, ((0, 8), (1, 2)), jnp.float32)
    child_panel = scatter_about(part_keys[2], (NS, NC * W), NS ** -0.5, 0.0546875, ((0, 8), (1, 2)), jnp.float32)
    child_link = scatter_about(part_keys[3], (NC, W, W), W ** -0.5, 0.5, ((0, 2),), jnp.float32)
    parent_pivot_inv = scatter_about(part_keys[4], (NP, W, W), 1.0, 6.0, ((0, 2),), jnp.float32)
    child_pivot_inv = scatter_about(part_keys[5], (NC, W, W), 1.0, 6.0, ((0, 2),), jnp.float32)
    parent_blocks = plant((jax.random.randint(part_keys[6], (NP, NB), 0, 4) < 3).astype(jnp.int32), jax.random.fold_in(part_keys[6], 1), 0, 1)
    child_blocks = plant((jax.random.randint(part_keys[7], (NC, NB), 0, 4) < 3).astype(jnp.int32), jax.random.fold_in(part_keys[7], 1), 0, 1)
    tree = draw_tree(jax.random.fold_in(jax.random.fold_in(seeds[9], part), 71), part)
    return dict(ancestor_inverse=ancestor_inverse, parent_panel=parent_panel, child_panel=child_panel, child_link=child_link, parent_pivot_inv=parent_pivot_inv, child_pivot_inv=child_pivot_inv, parent_blocks=parent_blocks, child_blocks=child_blocks, tree=tree)


HIGH = lax.Precision.HIGHEST


def expand_mask(mask_rows):
    table = mask_rows.T.astype(jnp.float32)
    return jnp.repeat(jnp.repeat(table, W, axis=0), W, axis=1)


def reference(ancestor_inverse, parent_panel, child_panel, child_link, parent_pivot_inv, child_pivot_inv, parent_blocks, child_blocks, tree):
    parent_masked = parent_panel * expand_mask(parent_blocks)
    parent_column = -jnp.dot(ancestor_inverse, parent_masked, precision=HIGH, preferred_element_type=jnp.float32)
    masked_three = parent_masked.reshape(NS, NP, W)
    column_three = parent_column.reshape(NS, NP, W)
    parent_diag = parent_pivot_inv - jnp.einsum("snw,snv->nwv", masked_three, column_three, precision=HIGH)
    child_mask = parent_blocks[tree] * child_blocks
    child_masked = child_panel * expand_mask(child_mask)
    child_three = child_masked.reshape(NS, NC, W)
    selected = column_three[:, tree, :]
    product = jnp.dot(ancestor_inverse, child_masked, precision=HIGH, preferred_element_type=jnp.float32).reshape(NS, NC, W)
    child_col3 = -(product + jnp.einsum("scw,cwv->scv", selected, child_link, precision=HIGH))
    child_cross = -(jnp.einsum("scw,scv->cwv", selected, child_three, precision=HIGH) + jnp.einsum("cwu,cuv->cwv", parent_diag[tree], child_link, precision=HIGH))
    child_diag = child_pivot_inv - jnp.einsum("scw,scv->cwv", child_three, child_col3, precision=HIGH) - jnp.einsum("cuw,cuv->cwv", child_link, child_cross, precision=HIGH)
    return parent_column, parent_diag, child_col3.reshape(NS, NC * W), child_cross, child_diag
```

```python
import functools

import jax
import jax.numpy as jnp
from jax import lax
from jax.experimental import pallas as pl
from jax.experimental.pallas import tpu as pltpu
from jax.sharding import PartitionSpec as P

HIGH = lax.Precision.HIGHEST
MESH = pl.DeviceIdType.MESH
LAG = 2


def expand_mask(mask_rows, width):
    table = mask_rows.T.astype(jnp.float32)
    return jnp.repeat(jnp.repeat(table, width, axis=0), width, axis=1)


def split(value):
    high = value.astype(jnp.bfloat16)
    return high, (value - high.astype(jnp.float32)).astype(jnp.bfloat16)


def dot_split(left, right):
    lh, ll = left
    rh, rl = right
    dot = functools.partial(jnp.dot, preferred_element_type=jnp.float32)
    return dot(lh, rh) + (dot(lh, rl) + dot(ll, rh))


def dot3(left, right):
    return dot_split(split(left), split(right))


def kernel(
    geo, tree_ref, own_ref, a_ref, link_ref, pivot_ref,
    pcol_ref, ccol_ref, part_ref, pick_ref,
    panel, acc, a_buf, halves, other, pivots,
    own_sem, sib_send, sib_recv, recv, send, a_sem, ex_send, ex_recv, pv_send, pv_recv,
):
    deep, wide, rows, piece, tile, w = geo
    half, cuts, tiles = deep // 2, rows // piece, rows // tile
    own_slot = half * wide
    count = half * cuts
    row, c = lax.axis_index("row"), lax.axis_index("col")
    z, y = row // wide, row % wide
    m = z + c * (deep - 1 - 2 * z)
    sibling = {"row": row, "col": 1 - c}

    def row_at(place, column):
        return (place + c * (deep - 1 - 2 * place)) * wide + column

    def local(source, column):
        return (source + c * (half - 1 - 2 * source)) * wide + column

    def source_of(j):
        left, right = m, half - 1 - m
        both = jnp.minimum(left, right)
        step = (j + 1) // 2
        near = m + jnp.where(j % 2 == 1, step, -step)
        far = jnp.where(left > right, m - (j - both), m + (j - both))
        inside = jnp.where(j <= 2 * both, near, far)
        return jnp.where(m >= half, half - 1 - j, inside)

    has_right, has_left = m + 1 < deep, m >= 1
    barrier = pltpu.get_barrier_semaphore()
    pl.semaphore_signal(barrier, inc=1, device_id=sibling, device_id_type=MESH)

    @pl.when(has_right)
    def _():
        pl.semaphore_signal(
            barrier, inc=1, device_id={"row": row_at(m + 1, y), "col": c}, device_id_type=MESH
        )

    @pl.when(has_left)
    def _():
        pl.semaphore_signal(
            barrier, inc=1, device_id={"row": row_at(m - 1, y), "col": c}, device_id_type=MESH
        )

    if wide == 2:
        pl.semaphore_signal(
            barrier, inc=1, device_id={"row": row_at(m, 1 - y), "col": c}, device_id_type=MESH
        )

    own_lanes = pl.ds(pl.multiple_of(c * 2 * w, 2 * w), 2 * w)

    def own_copy():
        return pltpu.make_async_copy(own_ref, panel.at[own_slot, :, own_lanes], own_sem)

    def sib_copy(q):
        at = pl.ds(pl.multiple_of(q * piece, piece), piece)
        return pltpu.make_async_remote_copy(
            src_ref=own_ref.at[at],
            dst_ref=panel.at[own_slot, at, own_lanes],
            send_sem=sib_send.at[q],
            recv_sem=sib_recv.at[q],
            device_id=sibling,
            device_id_type=MESH,
        )

    def pivot_copy():
        return pltpu.make_async_remote_copy(
            src_ref=pivot_ref,
            dst_ref=pivots,
            send_sem=pv_send,
            recv_sem=pv_recv,
            device_id=sibling,
            device_id_type=MESH,
        )

    def where_is(i, column):
        source, q = source_of(i // cuts), i % cuts
        return source, q, local(source, column)

    def a_copy(kind, i):
        column = y if kind == 0 else 1 - y
        _, q, slot = where_is(i, column)
        at = pl.ds(pl.multiple_of(slot * rows + q * piece, piece), piece)
        return pltpu.make_async_copy(
            a_ref.at[:, at], a_buf.at[kind, i % 2], a_sem.at[kind, i % 2]
        )

    def forward(way, i):
        source, q, slot = where_is(i, y)
        here = jnp.where(source == m, own_slot, slot)
        at = pl.ds(pl.multiple_of(q * piece, piece), piece)
        target = (row_at(m + 1, y), row_at(m - 1, y), row_at(m, 1 - y))[way]
        return pltpu.make_async_remote_copy(
            src_ref=panel.at[here, at],
            dst_ref=panel.at[slot, at],
            send_sem=send.at[way, i],
            recv_sem=recv.at[slot * cuts + q],
            device_id={"row": target, "col": c},
            device_id_type=MESH,
        )

    def each_forward(i, act):
        source, _, _ = where_is(i, y)

        @pl.when(has_right & (source <= m))
        def _():
            act(forward(0, i))

        @pl.when(has_left & (source >= m))
        def _():
            act(forward(1, i))

        if wide == 2:
            act(forward(2, i))

    def arrived(slot, q):
        at = pl.ds(pl.multiple_of(q * piece, piece), piece)
        pltpu.make_async_remote_copy(
            src_ref=panel.at[slot, at],
            dst_ref=panel.at[slot, at],
            send_sem=send.at[0, 0],
            recv_sem=recv.at[slot * cuts + q],
            device_id=sibling,
            device_id_type=MESH,
        ).wait_recv()

    def multiply(slot, q, kind, i):
        at = pl.ds(pl.multiple_of(q * piece, piece), piece)
        halves[0], halves[1] = split(panel[slot, at])

        def one(t, carry):
            r = pl.ds(pl.multiple_of(t * tile, tile), tile)
            left = split(a_buf[kind, i % 2, r])
            acc[r] += dot_split(left, (halves[0], halves[1]))
            return carry

        lax.fori_loop(0, tiles, one, 0)

    a_copy(0, 0).start()
    if wide == 2:
        a_copy(1, 0).start()
    own_copy().start()
    acc[...] = jnp.zeros_like(acc)
    part_ref[...] = jnp.zeros_like(part_ref)
    greeted = 1 + (wide == 2) + has_right.astype(jnp.int32) + has_left.astype(jnp.int32)
    pl.semaphore_wait(barrier, greeted)

    def start_sib(q, carry):
        sib_copy(q).start()
        return carry

    lax.fori_loop(0, cuts, start_sib, 0)
    pivot_copy().start()
    own_copy().wait()

    def step(i, carry):
        @pl.when(i < count)
        def _():
            source, q, slot = where_is(i, y)
            mine = source == m

            @pl.when(mine)
            def _():
                sib_copy(q).wait_recv()

            @pl.when(jnp.logical_not(mine))
            def _():
                arrived(slot, q)

            each_forward(i, lambda copy: copy.start())
            a_copy(0, i).wait()

            @pl.when(i + 1 < count)
            def _():
                a_copy(0, i + 1).start()

            multiply(jnp.where(mine, own_slot, slot), q, 0, i)

        if wide == 2:

            @pl.when(i >= LAG)
            def _():
                t = i - LAG
                _, q, slot = where_is(t, 1 - y)
                arrived(slot, q)
                a_copy(1, t).wait()

                @pl.when(t + 1 < count)
                def _():
                    a_copy(1, t + 1).start()

                multiply(slot, q, 1, t)

        return carry

    lax.fori_loop(0, count + (LAG if wide == 2 else 0), step, 0)

    def ex_copy(t, which):
        r = pl.ds(pl.multiple_of(t * tile, tile), tile)
        lanes = (0, 2 * w, (1 - c) * 2 * w + w)[which]
        lanes = pl.ds(pl.multiple_of(lanes, w), w)
        return pltpu.make_async_remote_copy(
            src_ref=acc.at[r, lanes],
            dst_ref=other.at[which, r],
            send_sem=ex_send.at[t, which],
            recv_sem=ex_recv.at[t, which],
            device_id=sibling,
            device_id_type=MESH,
        )

    def ex_start(t, carry):
        for which in range(3):
            ex_copy(t, which).start()
        return carry

    lax.fori_loop(0, tiles, ex_start, 0)

    @pl.when(m >= half)
    def _():
        def sib_wait(q, carry):
            sib_copy(q).wait_recv()
            return carry

        lax.fori_loop(0, cuts, sib_wait, 0)

    pick = tree_ref[c].astype(jnp.float32)
    side = c.astype(jnp.float32)

    def choose(by, first, second):
        return first * (1.0 - by) + second * by

    link = split(link_ref[0])

    def tail(t, carry):
        r = pl.ds(pl.multiple_of(t * tile, tile), tile)
        for which in range(3):
            ex_copy(t, which).wait_recv()
        p0 = -(acc[r, 0:w] + other[0, r])
        p1 = -(acc[r, 2 * w : 3 * w] + other[1, r])
        total = choose(side, acc[r, w : 2 * w], acc[r, 3 * w : 4 * w]) + other[2, r]
        chip = panel[own_slot, r]
        m0, m1 = chip[:, 0:w], chip[:, 2 * w : 3 * w]
        kids = choose(side, chip[:, w : 2 * w], chip[:, 3 * w :])
        pcol = choose(side, p0, p1)
        chosen = choose(pick, p0, p1)
        ccol = -(total + dot_split(split(chosen), link))
        pcol_ref[r] = pcol
        ccol_ref[r] = ccol
        own_t = split(choose(side, m0, m1).T)
        pick_t = split(choose(pick, m0, m1).T)
        kids_t = split(kids.T)
        part_ref[0] += dot_split(own_t, split(pcol))
        part_ref[1] += dot_split(pick_t, split(chosen))
        part_ref[2] += dot_split(split(chosen.T), split(kids))
        part_ref[3] += dot_split(kids_t, split(ccol))
        return carry

    lax.fori_loop(0, tiles, tail, 0)

    pivot_copy().wait()
    first = choose(side, pivot_ref[0], pivots[0])
    second = choose(side, pivots[0], pivot_ref[0])
    pick_ref[...] = choose(pick, first, second)

    def drain(i, carry):
        each_forward(i, lambda copy: copy.wait_send())
        return carry

    lax.fori_loop(0, count, drain, 0)

    def drain_sib(q, carry):
        sib_copy(q).wait_send()
        return carry

    lax.fori_loop(0, cuts, drain_sib, 0)

    def drain_ex(t, carry):
        for which in range(3):
            ex_copy(t, which).wait_send()
        return carry

    lax.fori_loop(0, tiles, drain_ex, 0)


def columns(wide, tree, own, ancestor_inverse, link, pivot):
    rows, w = own.shape[0], link.shape[1]
    line = lax.axis_size("row") // wide
    piece = 256 if rows % 256 == 0 else 128
    tile = piece
    half, cuts, tiles = line // 2, rows // piece, rows // piece
    count = half * cuts
    f32 = jnp.float32
    vmem = pl.BlockSpec(memory_space=pltpu.VMEM)
    anywhere = pl.BlockSpec(memory_space=pl.ANY)
    dma = pltpu.SemaphoreType.DMA
    flops = 2 * rows * ancestor_inverse.shape[1] * 4 * w * 3
    return pl.pallas_call(
        functools.partial(kernel, (line, wide, rows, piece, tile, w)),
        out_shape=(
            jax.ShapeDtypeStruct((rows, w), f32),
            jax.ShapeDtypeStruct((rows, w), f32),
            jax.ShapeDtypeStruct((4, w, w), f32),
            jax.ShapeDtypeStruct((w, w), f32),
        ),
        in_specs=[pl.BlockSpec(memory_space=pltpu.SMEM), anywhere, anywhere, vmem, vmem],
        out_specs=(vmem, vmem, vmem, vmem),
        scratch_shapes=[
            pltpu.VMEM((half * wide + 1, rows, 4 * w), f32),
            pltpu.VMEM((rows, 4 * w), f32),
            pltpu.VMEM((wide, 2, rows, piece), f32),
            pltpu.VMEM((2, piece, 4 * w), jnp.bfloat16),
            pltpu.VMEM((3, rows, w), f32),
            pltpu.VMEM((1, w, w), f32),
            dma,
            dma((cuts,)),
            dma((cuts,)),
            dma((half * wide * cuts,)),
            dma((3, count)),
            dma((wide, 2)),
            dma((tiles, 3)),
            dma((tiles, 3)),
            dma,
            dma,
        ],
        cost_estimate=pl.CostEstimate(
            flops=flops, bytes_accessed=4 * ancestor_inverse.size, transcendentals=0
        ),
        compiler_params=pltpu.CompilerParams(
            collective_id=0, has_side_effects=True, vmem_limit_bytes=48 * 2**20
        ),
    )(tree, own, ancestor_inverse, link, pivot)


def per_device(
    wide,
    ancestor_inverse,
    parent_panel,
    child_panel,
    child_link,
    parent_pivot_inv,
    child_pivot_inv,
    parent_blocks,
    child_blocks,
    tree,
):
    width = child_link.shape[1]
    rows = ancestor_inverse.shape[0]
    row_index = lax.axis_index("row")
    col_index = lax.axis_index("col")
    here = rows // width
    start = row_index * here
    parents = lax.dynamic_slice_in_dim(parent_blocks, start, here, 1)
    kept = lax.dynamic_slice(child_blocks, (col_index, start), (1, here))
    parent_mask = lax.dynamic_slice_in_dim(parents, col_index, 1, 0)
    mine = lax.dynamic_slice_in_dim(tree, col_index, 1, 0)
    inherited = jnp.where(mine[:, None] == 0, parents[0:1], parents[1:2])
    own = jnp.concatenate(
        [
            parent_panel * expand_mask(parent_mask, width),
            child_panel * expand_mask(inherited * kept, width),
        ],
        axis=1,
    )
    pcol, ccol, part, pick = columns(
        wide, tree, own, ancestor_inverse, child_link, parent_pivot_inv
    )
    total = lax.psum(part, "row")
    parent_diag = parent_pivot_inv - total[0:1]
    link = child_link[0]
    dot = functools.partial(jnp.dot, precision=HIGH, preferred_element_type=jnp.float32)
    cross = -(total[2] + dot(pick - total[1], link))
    diag = child_pivot_inv - total[3:4] - dot(link.T, cross)[None]
    return pcol, parent_diag, ccol, cross[None], diag


def solution(mesh):
    line = list(mesh.devices[0, :, 0])
    places = {getattr(device, "coords", (0, index % 2, 0))[1] for index, device in enumerate(line)}
    wide = 2 if len(places) == 2 else 1
    return jax.shard_map(
        functools.partial(per_device, wide),
        mesh=mesh,
        in_specs=(
            P(("pole", "row"), "col"),
            P(("pole", "row"), "col"),
            P(("pole", "row"), "col"),
            P(("pole", "col"), None, None),
            P(("pole", "col"), None, None),
            P(("pole", "col"), None, None),
            P("pole", None),
            P("pole", None),
            P("pole"),
        ),
        out_specs=(
            P(("pole", "row"), "col"),
            P(("pole", "col"), None, None),
            P(("pole", "row"), "col"),
            P(("pole", "col"), None, None),
            P(("pole", "col"), None, None),
        ),
        check_vma=False,
    )
```

```python
import functools

import jax
import jax.numpy as jnp
from jax import lax
from jax.experimental import pallas as pl
from jax.experimental.pallas import tpu as pltpu
from jax.sharding import PartitionSpec as P

MESH = pl.DeviceIdType.MESH
LAG = 2


def split(value):
    high = value.astype(jnp.bfloat16)
    return high, (value - high.astype(jnp.float32)).astype(jnp.bfloat16)


def dot_split(left, right):
    lh, ll = left
    rh, rl = right
    dot = functools.partial(jnp.dot, preferred_element_type=jnp.float32)
    return dot(lh, rh) + (dot(lh, rl) + dot(ll, rh))


def dot3(left, right):
    return dot_split(split(left), split(right))


def kernel(
    geo, tree_ref, parents_ref, kids_ref, parent_ref, child_ref, a_ref,
    link_ref, pivot_ref, child_pivot_ref,
    pcol_ref, pdiag_ref, ccol_ref, cross_ref, cdiag_ref,
    panel, acc, a_buf, halves, other, pivots, raw, part, terms, whole,
    own_sem, sib_send, sib_recv, recv, send, a_sem, ex_send, ex_recv, pv_send, pv_recv,
    rs_send, rs_recv, ag_send, ag_recv,
):
    deep, wide, rows, piece, tile, w = geo
    line = deep * wide
    share = 4 * w // line
    half, cuts, tiles = deep // 2, rows // piece, rows // tile
    own_slot = half * wide
    count = half * cuts
    row, c = lax.axis_index("row"), lax.axis_index("col")
    z, y = row // wide, row % wide
    m = z + c * (deep - 1 - 2 * z)
    sibling = {"row": row, "col": 1 - c}

    def row_at(place, column):
        return (place + c * (deep - 1 - 2 * place)) * wide + column

    def local(source, column):
        return (source + c * (half - 1 - 2 * source)) * wide + column

    def source_of(j):
        left, right = m, half - 1 - m
        both = jnp.minimum(left, right)
        step = (j + 1) // 2
        near = m + jnp.where(j % 2 == 1, step, -step)
        far = jnp.where(left > right, m - (j - both), m + (j - both))
        inside = jnp.where(j <= 2 * both, near, far)
        return jnp.where(m >= half, half - 1 - j, inside)

    has_right, has_left = m + 1 < deep, m >= 1
    barrier = pltpu.get_barrier_semaphore()
    pl.semaphore_signal(barrier, inc=1, device_id=sibling, device_id_type=MESH)

    def greet(k, carry):
        pl.semaphore_signal(
            barrier, inc=1, device_id={"row": (row + k) % line, "col": c}, device_id_type=MESH
        )
        return carry

    lax.fori_loop(1, line, greet, 0)
    own_lanes = pl.ds(pl.multiple_of(c * 2 * w, 2 * w), 2 * w)

    def raw_copy(which):
        return pltpu.make_async_copy((parent_ref, child_ref)[which], raw.at[which], own_sem.at[which])

    def sib_copy(q):
        at = pl.ds(pl.multiple_of(q * piece, piece), piece)
        return pltpu.make_async_remote_copy(
            src_ref=panel.at[own_slot, at, own_lanes],
            dst_ref=panel.at[own_slot, at, own_lanes],
            send_sem=sib_send.at[q],
            recv_sem=sib_recv.at[q],
            device_id=sibling,
            device_id_type=MESH,
        )

    def pivot_copy():
        return pltpu.make_async_remote_copy(
            src_ref=pivot_ref,
            dst_ref=pivots,
            send_sem=pv_send,
            recv_sem=pv_recv,
            device_id=sibling,
            device_id_type=MESH,
        )

    def where_is(i, column):
        source, q = source_of(i // cuts), i % cuts
        return source, q, local(source, column)

    def a_copy(kind, i):
        column = y if kind == 0 else 1 - y
        _, q, slot = where_is(i, column)
        at = pl.ds(pl.multiple_of(slot * rows + q * piece, piece), piece)
        return pltpu.make_async_copy(
            a_ref.at[:, at], a_buf.at[kind, i % 2], a_sem.at[kind, i % 2]
        )

    def forward(way, i):
        source, q, slot = where_is(i, y)
        here = jnp.where(source == m, own_slot, slot)
        at = pl.ds(pl.multiple_of(q * piece, piece), piece)
        target = (row_at(m + 1, y), row_at(m - 1, y), row_at(m, 1 - y))[way]
        return pltpu.make_async_remote_copy(
            src_ref=panel.at[here, at],
            dst_ref=panel.at[slot, at],
            send_sem=send.at[way, i],
            recv_sem=recv.at[slot * cuts + q],
            device_id={"row": target, "col": c},
            device_id_type=MESH,
        )

    def each_forward(i, act):
        source, _, _ = where_is(i, y)

        @pl.when(has_right & (source <= m))
        def _():
            act(forward(0, i))

        @pl.when(has_left & (source >= m))
        def _():
            act(forward(1, i))

        if wide == 2:
            act(forward(2, i))

    def arrived(slot, q):
        at = pl.ds(pl.multiple_of(q * piece, piece), piece)
        pltpu.make_async_remote_copy(
            src_ref=panel.at[slot, at],
            dst_ref=panel.at[slot, at],
            send_sem=send.at[0, 0],
            recv_sem=recv.at[slot * cuts + q],
            device_id=sibling,
            device_id_type=MESH,
        ).wait_recv()

    def multiply(slot, q, kind, i, then=None):
        at = pl.ds(pl.multiple_of(q * piece, piece), piece)
        halves[0], halves[1] = split(panel[slot, at])

        def one(t, carry):
            r = pl.ds(pl.multiple_of(t * tile, tile), tile)
            left = split(a_buf[kind, i % 2, r])
            acc[r] += dot_split(left, (halves[0], halves[1]))
            if then is not None:
                then(t)
            return carry

        lax.fori_loop(0, tiles, one, 0)

    a_copy(0, 0).start()
    if wide == 2:
        a_copy(1, 0).start()
    raw_copy(0).start()
    raw_copy(1).start()
    acc[...] = jnp.zeros_like(acc)
    part[...] = jnp.zeros_like(part)
    tree = tree_ref[c]
    raw_copy(0).wait()
    raw_copy(1).wait()
    for b in range(rows // w):
        at = slice(b * w, (b + 1) * w)
        spot = row * (rows // w) + b
        inherited = parents_ref[0, spot] * (1 - tree) + parents_ref[1, spot] * tree
        keep_parent = parents_ref[c, spot].astype(jnp.float32)
        keep_child = (inherited * kids_ref[c, spot]).astype(jnp.float32)
        for core in range(2):

            @pl.when(c == core)
            def _(core=core, at=at, keep_parent=keep_parent, keep_child=keep_child):
                first = core * 2 * w
                panel[own_slot, at, first : first + w] = raw[0, at] * keep_parent
                panel[own_slot, at, first + w : first + 2 * w] = raw[1, at] * keep_child

    pl.semaphore_wait(barrier, line)

    def start_sib(q, carry):
        sib_copy(q).start()
        return carry

    lax.fori_loop(0, cuts, start_sib, 0)
    pivot_copy().start()

    def ex_copy(t, which):
        r = pl.ds(pl.multiple_of(t * tile, tile), tile)
        lanes = (0, 2 * w, (1 - c) * 2 * w + w)[which]
        lanes = pl.ds(pl.multiple_of(lanes, w), w)
        return pltpu.make_async_remote_copy(
            src_ref=acc.at[r, lanes],
            dst_ref=other.at[which, r],
            send_sem=ex_send.at[t, which],
            recv_sem=ex_recv.at[t, which],
            device_id=sibling,
            device_id_type=MESH,
        )

    def ex_start(t):
        for which in range(3):
            ex_copy(t, which).start()

    def own_step(i, then=None):
        source, q, slot = where_is(i, y)
        mine = source == m

        @pl.when(mine)
        def _():
            sib_copy(q).wait_recv()

        @pl.when(jnp.logical_not(mine))
        def _():
            arrived(slot, q)

        each_forward(i, lambda copy: copy.start())
        a_copy(0, i).wait()

        @pl.when(i + 1 < count)
        def _():
            a_copy(0, i + 1).start()

        multiply(jnp.where(mine, own_slot, slot), q, 0, i, then)

    def other_step(t, then=None):
        _, q, slot = where_is(t, 1 - y)
        arrived(slot, q)
        a_copy(1, t).wait()

        @pl.when(t + 1 < count)
        def _():
            a_copy(1, t + 1).start()

        multiply(slot, q, 1, t, then)

    def step(i, carry):
        if wide == 2:

            @pl.when(i < count)
            def _():
                own_step(i)

            @pl.when(i >= LAG)
            def _():
                other_step(i - LAG)

        else:
            own_step(i)
        return carry

    if wide == 2:
        lax.fori_loop(0, count + LAG - 1, step, 0)
        other_step(count - 1, ex_start)
    else:
        lax.fori_loop(0, count - 1, step, 0)
        own_step(count - 1, ex_start)

    @pl.when(m >= half)
    def _():
        def sib_wait(q, carry):
            sib_copy(q).wait_recv()
            return carry

        lax.fori_loop(0, cuts, sib_wait, 0)

    pick = tree.astype(jnp.float32)
    side = c.astype(jnp.float32)

    def choose(by, first, second):
        return first * (1.0 - by) + second * by

    link = split(link_ref[0])

    def tail(t, carry):
        r = pl.ds(pl.multiple_of(t * tile, tile), tile)
        for which in range(3):
            ex_copy(t, which).wait_recv()
        p0 = -(acc[r, 0:w] + other[0, r])
        p1 = -(acc[r, 2 * w : 3 * w] + other[1, r])
        total = choose(side, acc[r, w : 2 * w], acc[r, 3 * w : 4 * w]) + other[2, r]
        chip = panel[own_slot, r]
        m0, m1 = chip[:, 0:w], chip[:, 2 * w : 3 * w]
        kids = choose(side, chip[:, w : 2 * w], chip[:, 3 * w :])
        pcol = choose(side, p0, p1)
        chosen = choose(pick, p0, p1)
        ccol = -(total + dot_split(split(chosen), link))
        pcol_ref[r] = pcol
        ccol_ref[r] = ccol
        own_t = split(choose(side, m0, m1).T)
        pick_t = split(choose(pick, m0, m1).T)
        kids_t = split(kids.T)
        part[0 * w : 1 * w] += dot_split(own_t, split(pcol))
        part[1 * w : 2 * w] += dot_split(pick_t, split(chosen))
        part[2 * w : 3 * w] += dot_split(split(chosen.T), split(kids))
        part[3 * w : 4 * w] += dot_split(kids_t, split(ccol))
        return carry

    lax.fori_loop(0, tiles, tail, 0)

    def shares(place):
        return pl.ds(pl.multiple_of(place * share, share), share)

    def rs_copy(k):
        to = (row + k) % line
        return pltpu.make_async_remote_copy(
            src_ref=part.at[shares(to)],
            dst_ref=terms.at[k],
            send_sem=rs_send.at[k],
            recv_sem=rs_recv.at[k],
            device_id={"row": to, "col": c},
            device_id_type=MESH,
        )

    def ag_copy(k):
        return pltpu.make_async_remote_copy(
            src_ref=whole.at[shares(row)],
            dst_ref=whole.at[shares(row)],
            send_sem=ag_send.at[k],
            recv_sem=ag_recv.at[k],
            device_id={"row": (row + k) % line, "col": c},
            device_id_type=MESH,
        )

    def ag_arrived(k):
        start = shares((row + line - k) % line)
        pltpu.make_async_remote_copy(
            src_ref=whole.at[start],
            dst_ref=whole.at[start],
            send_sem=ag_send.at[k],
            recv_sem=ag_recv.at[k],
            device_id=sibling,
            device_id_type=MESH,
        ).wait_recv()

    def loop(body):
        def one(k, carry):
            body(k)
            return carry

        lax.fori_loop(1, line, one, 0)

    loop(lambda k: rs_copy(k).start())

    def add_term(k, total):
        rs_copy(k).wait_recv()
        return total + terms[k]

    whole[shares(row)] = lax.fori_loop(1, line, add_term, part[shares(row)])
    loop(lambda k: ag_copy(k).start())
    pivot_copy().wait()
    first = choose(side, pivot_ref[0], pivots[0])
    second = choose(side, pivots[0], pivot_ref[0])
    chosen_pivot = choose(pick, first, second)
    loop(ag_arrived)
    pdiag_ref[0] = pivot_ref[0] - whole[0:w]
    cross = -(whole[2 * w : 3 * w] + dot_split(split(chosen_pivot - whole[w : 2 * w]), link))
    cross_ref[0] = cross
    cdiag_ref[0] = child_pivot_ref[0] - whole[3 * w :] - dot3(link_ref[0].T, cross)
    loop(lambda k: rs_copy(k).wait_send())
    loop(lambda k: ag_copy(k).wait_send())

    def drain(i, carry):
        each_forward(i, lambda copy: copy.wait_send())
        return carry

    lax.fori_loop(0, count, drain, 0)

    def drain_sib(q, carry):
        sib_copy(q).wait_send()
        return carry

    lax.fori_loop(0, cuts, drain_sib, 0)

    def drain_ex(t, carry):
        for which in range(3):
            ex_copy(t, which).wait_send()
        return carry

    lax.fori_loop(0, tiles, drain_ex, 0)


def per_device(
    wide,
    ancestor_inverse,
    parent_panel,
    child_panel,
    child_link,
    parent_pivot_inv,
    child_pivot_inv,
    parent_blocks,
    child_blocks,
    tree,
):
    rows, w = ancestor_inverse.shape[0], child_link.shape[1]
    whole_line = lax.axis_size("row")
    line = whole_line // wide
    piece = 256 if rows % 256 == 0 else 128
    tile = piece
    half, cuts, tiles = line // 2, rows // piece, rows // piece
    count = half * cuts
    f32 = jnp.float32
    scalars = pl.BlockSpec(memory_space=pltpu.SMEM)
    vmem = pl.BlockSpec(memory_space=pltpu.VMEM)
    anywhere = pl.BlockSpec(memory_space=pl.ANY)
    dma = pltpu.SemaphoreType.DMA
    flops = 2 * rows * ancestor_inverse.shape[1] * 4 * w * 3
    return pl.pallas_call(
        functools.partial(kernel, (line, wide, rows, piece, tile, w)),
        out_shape=(
            jax.ShapeDtypeStruct((rows, w), f32),
            jax.ShapeDtypeStruct((1, w, w), f32),
            jax.ShapeDtypeStruct((rows, w), f32),
            jax.ShapeDtypeStruct((1, w, w), f32),
            jax.ShapeDtypeStruct((1, w, w), f32),
        ),
        in_specs=[scalars] * 3 + [anywhere] * 3 + [vmem] * 3,
        out_specs=(vmem,) * 5,
        scratch_shapes=[
            pltpu.VMEM((half * wide + 1, rows, 4 * w), f32),
            pltpu.VMEM((rows, 4 * w), f32),
            pltpu.VMEM((wide, 2, rows, piece), f32),
            pltpu.VMEM((2, piece, 4 * w), jnp.bfloat16),
            pltpu.VMEM((3, rows, w), f32),
            pltpu.VMEM((1, w, w), f32),
            pltpu.VMEM((2, rows, w), f32),
            pltpu.VMEM((4 * w, w), f32),
            pltpu.VMEM((whole_line, 4 * w // whole_line, w), f32),
            pltpu.VMEM((4 * w, w), f32),
            dma((2,)),
            dma((cuts,)),
            dma((cuts,)),
            dma((half * wide * cuts,)),
            dma((3, count)),
            dma((wide, 2)),
            dma((tiles, 3)),
            dma((tiles, 3)),
            dma,
            dma,
            dma((whole_line,)),
            dma((whole_line,)),
            dma((whole_line,)),
            dma((whole_line,)),
        ],
        cost_estimate=pl.CostEstimate(
            flops=flops, bytes_accessed=4 * ancestor_inverse.size, transcendentals=0
        ),
        compiler_params=pltpu.CompilerParams(
            collective_id=0, has_side_effects=True, vmem_limit_bytes=48 * 2**20
        ),
    )(
        tree,
        parent_blocks,
        child_blocks,
        parent_panel,
        child_panel,
        ancestor_inverse,
        child_link,
        parent_pivot_inv,
        child_pivot_inv,
    )


def solution(mesh):
    line = list(mesh.devices[0, :, 0])
    places = {getattr(device, "coords", (0, index % 2, 0))[1] for index, device in enumerate(line)}
    wide = 2 if len(places) == 2 else 1
    return jax.shard_map(
        functools.partial(per_device, wide),
        mesh=mesh,
        in_specs=(
            P(("pole", "row"), "col"),
            P(("pole", "row"), "col"),
            P(("pole", "row"), "col"),
            P(("pole", "col"), None, None),
            P(("pole", "col"), None, None),
            P(("pole", "col"), None, None),
            P("pole", None),
            P("pole", None),
            P("pole"),
        ),
        out_specs=(
            P(("pole", "row"), "col"),
            P(("pole", "col"), None, None),
            P(("pole", "row"), "col"),
            P(("pole", "col"), None, None),
            P(("pole", "col"), None, None),
        ),
        check_vma=False,
    )
```

```python
import functools

import jax
import jax.numpy as jnp
from jax import lax
from jax.experimental import pallas as pl
from jax.experimental.pallas import tpu as pltpu
from jax.sharding import PartitionSpec as P

MESH = pl.DeviceIdType.MESH
LAG = 4


def split(value):
    high = value.astype(jnp.bfloat16)
    return high, (value - high.astype(jnp.float32)).astype(jnp.bfloat16)


def dot_split(left, right):
    lh, ll = left
    rh, rl = right
    dot = functools.partial(jnp.dot, preferred_element_type=jnp.float32)
    return dot(lh, rh) + (dot(lh, rl) + dot(ll, rh))


def dot3(left, right):
    return dot_split(split(left), split(right))


class RowSum:
    def __init__(self, line, share, part, terms, whole, sems):
        self.line, self.share, self.part, self.terms, self.whole = line, share, part, terms, whole
        self.sems = sems
        self.owners = part.shape[0] // share
        self.row, self.c = lax.axis_index("row"), lax.axis_index("col")

    def at(self, place):
        return pl.ds(pl.multiple_of(place * self.share, self.share), self.share)

    def copy(self, k, stage, src, dst):
        return pltpu.make_async_remote_copy(
            src_ref=src,
            dst_ref=dst,
            send_sem=self.sems.at[2 * stage, k],
            recv_sem=self.sems.at[2 * stage + 1, k],
            device_id={"row": (self.row + k) % self.line, "col": self.c},
            device_id_type=MESH,
        )

    def scatter(self, k):
        to = (self.row + k) % self.line
        return self.copy(k, 0, self.part.at[self.at(to)], self.terms.at[k])

    def gather(self, k):
        return self.copy(k, 1, self.whole.at[self.at(self.row)], self.whole.at[self.at(self.row)])

    def guard(self, place, act):
        if self.owners == self.line:
            act()
        else:
            pl.when(place < self.owners)(act)

    def loop(self, body):
        def one(k, carry):
            body(k)
            return carry

        lax.fori_loop(1, self.line, one, 0)

    def start(self):
        self.loop(
            lambda k: self.guard((self.row + k) % self.line, lambda: self.scatter(k).start())
        )

    def reduce(self):
        def act():
            def add_term(k, total):
                self.scatter(k).wait_recv()
                return total + self.terms[k]

            mine = self.at(self.row)
            self.whole[mine] = lax.fori_loop(1, self.line, add_term, self.part[mine])
            self.loop(lambda k: self.gather(k).start())

        self.guard(self.row, act)

    def finish(self):
        def one(k):
            origin = (self.row + self.line - k) % self.line
            spot = self.whole.at[self.at(origin)]
            self.guard(origin, lambda: self.copy(k, 1, spot, spot).wait_recv())

        self.loop(one)

    def drain(self):
        self.loop(
            lambda k: self.guard((self.row + k) % self.line, lambda: self.scatter(k).wait_send())
        )
        self.guard(self.row, lambda: self.loop(lambda k: self.gather(k).wait_send()))


def kernel(
    geo, tree_hbm, parents_hbm, kids_hbm, parent_ref, child_ref, a_ref,
    link_ref, pivot_ref, child_pivot_ref,
    pcol_ref, pdiag_ref, ccol_ref, cross_ref, cdiag_ref,
    tree_ref, parents_ref, kids_ref,
    panel, acc, a_buf, halves, other0, other1, raw, const, diags,
    part0, terms0, whole0, part1, terms1, whole1,
    in_sem, sib_send, sib_recv, recv, send, send_more, a_sem, ex_send, ex_recv, pd_sem,
    sems0, sems1,
):
    deep, wide, rows, piece, tile, w = geo
    line = deep * wide
    half, cuts, tiles = deep // 2, rows // piece, rows // tile
    own_slot = half * wide
    per = half * cuts
    count = 2 * per
    lag = LAG if wide == 2 else 0
    row, c = lax.axis_index("row"), lax.axis_index("col")
    z, y = row // wide, row % wide
    m = z + c * (deep - 1 - 2 * z)
    sibling = {"row": row, "col": 1 - c}
    sum0 = RowSum(line, 2 * w // line, part0, terms0, whole0, sems0)
    sum1 = RowSum(line, max(8, w // line), part1, terms1, whole1, sems1)

    def row_at(place, column):
        return (place + c * (deep - 1 - 2 * place)) * wide + column

    def local(source, column):
        return (source + c * (half - 1 - 2 * source)) * wide + column

    def source_of(j):
        left, right = m, half - 1 - m
        both = jnp.minimum(left, right)
        step = (j + 1) // 2
        near = m + jnp.where(j % 2 == 1, step, -step)
        far = jnp.where(left > right, m - (j - both), m + (j - both))
        inside = jnp.where(j <= 2 * both, near, far)
        return jnp.where(m >= half, half - 1 - j, inside)

    def cut(q):
        return pl.ds(pl.multiple_of(q * piece, piece), piece)

    def tile_at(t):
        return pl.ds(pl.multiple_of(t * tile, tile), tile)

    has_right, has_left = m + 1 < deep, m >= 1
    barrier = pltpu.get_barrier_semaphore()
    pl.semaphore_signal(barrier, inc=1, device_id=sibling, device_id_type=MESH)

    def greet(k, carry):
        pl.semaphore_signal(
            barrier, inc=1, device_id={"row": (row + k) % line, "col": c}, device_id_type=MESH
        )
        return carry

    lax.fori_loop(1, line, greet, 0)

    own_lanes = pl.ds(pl.multiple_of(c * w, w), w)

    def sib_copy(n):
        phase, at = n // cuts, cut(n % cuts)
        return pltpu.make_async_remote_copy(
            src_ref=raw.at[phase, at],
            dst_ref=panel.at[phase, own_slot, at, own_lanes],
            send_sem=sib_send.at[n],
            recv_sem=sib_recv.at[n],
            device_id=sibling,
            device_id_type=MESH,
        )

    def pd_copy():
        return pltpu.make_async_remote_copy(
            src_ref=diags.at[0],
            dst_ref=diags.at[1],
            send_sem=pd_sem.at[0],
            recv_sem=pd_sem.at[1],
            device_id=sibling,
            device_id_type=MESH,
        )

    def where_is(i, column):
        phase, rest = i // per, i % per
        source, q = source_of(rest // cuts), rest % cuts
        return phase, source, q, local(source, column)

    def flag(phase, slot, q):
        return (phase * half * wide + slot) * cuts + q

    def a_copy(kind, i):
        column = y if kind == 0 else 1 - y
        _, _, q, slot = where_is(i, column)
        at = pl.ds(pl.multiple_of(slot * rows + q * piece, piece), piece)
        return pltpu.make_async_copy(
            a_ref.at[:, at], a_buf.at[kind, i % 2], a_sem.at[kind, i % 2]
        )

    def hop(way, i, kind):
        column = y if kind == 0 else 1 - y
        phase, source, q, slot = where_is(i, column)
        here = jnp.where(source == m, own_slot, slot) if kind == 0 else slot
        target = (row_at(m + 1, y), row_at(m - 1, y), row_at(m, 1 - y))[way]
        return pltpu.make_async_remote_copy(
            src_ref=panel.at[phase, here, cut(q)],
            dst_ref=panel.at[phase, slot, cut(q)],
            send_sem=(send if kind == 0 else send_more).at[way, i],
            recv_sem=recv.at[flag(phase, slot, q)],
            device_id={"row": target, "col": c},
            device_id_type=MESH,
        )

    def each_hop(i, kind, act):
        _, source, q, _ = where_is(i, y)
        around = q == cuts - 1
        along = around if kind == 1 else True

        @pl.when(has_right & (source <= m) & along)
        def _():
            act(hop(0, i, kind))

        @pl.when(has_left & (source >= m) & along)
        def _():
            act(hop(1, i, kind))

        if wide == 2 and kind == 0:

            @pl.when(jnp.logical_not(around) | (source == m))
            def _():
                act(hop(2, i, kind))

    def arrived(phase, slot, q):
        spot = panel.at[phase, slot, cut(q)]
        pltpu.make_async_remote_copy(
            src_ref=spot,
            dst_ref=spot,
            send_sem=send.at[0, 0],
            recv_sem=recv.at[flag(phase, slot, q)],
            device_id=sibling,
            device_id_type=MESH,
        ).wait_recv()

    def ex_copy(phase, t):
        r = tile_at(t)
        if phase == 0:
            src, dst = acc.at[0, r], other0.at[r]
        else:
            lanes = pl.ds(pl.multiple_of((1 - c) * w, w), w)
            src, dst = acc.at[1, r, lanes], other1.at[r]
        return pltpu.make_async_remote_copy(
            src_ref=src,
            dst_ref=dst,
            send_sem=ex_send.at[phase, t],
            recv_sem=ex_recv.at[phase, t],
            device_id=sibling,
            device_id_type=MESH,
        )

    def multiply(phase, slot, q, kind, i, closes):
        halves[0], halves[1] = split(panel[phase, slot, cut(q)])

        def one(t, carry):
            r = tile_at(t)
            left = split(a_buf[kind, i % 2, r])
            acc[phase, r] += dot_split(left, (halves[0], halves[1]))
            if closes:

                @pl.when(i == per - 1)
                def _():
                    ex_copy(0, t).start()

                @pl.when(i == count - 1)
                def _():
                    ex_copy(1, t).start()

            return carry

        lax.fori_loop(0, tiles, one, 0)

    inputs = (
        (tree_hbm, tree_ref),
        (parents_hbm, parents_ref),
        (kids_hbm, kids_ref),
        (parent_ref, raw.at[0]),
        (child_ref, raw.at[1]),
        (link_ref.at[0], const.at[0]),
        (pivot_ref.at[0], const.at[1]),
        (child_pivot_ref.at[0], const.at[2]),
    )
    loads = [
        pltpu.make_async_copy(src, dst, in_sem.at[n]) for n, (src, dst) in enumerate(inputs)
    ]
    for load in loads:
        load.start()
    a_copy(0, 0).start()
    if wide == 2:
        a_copy(1, 0).start()
    for load in loads:
        load.wait()
    tree = tree_ref[c]
    for b in range(rows // w):
        at = slice(b * w, (b + 1) * w)
        spot = row * (rows // w) + b
        inherited = parents_ref[0, spot] * (1 - tree) + parents_ref[1, spot] * tree
        raw[0, at] = raw[0, at] * parents_ref[c, spot].astype(jnp.float32)
        raw[1, at] = raw[1, at] * (inherited * kids_ref[c, spot]).astype(jnp.float32)
    pl.semaphore_wait(barrier, line)

    def start_sib(n, carry):
        sib_copy(n).start()
        return carry

    lax.fori_loop(0, 2 * cuts, start_sib, 0)
    for core in range(2):

        @pl.when(c == core)
        def _(core=core):
            for phase in range(2):
                panel[phase, own_slot, :, core * w : (core + 1) * w] = raw[phase]

    acc[...] = jnp.zeros_like(acc)
    part0[...] = jnp.zeros_like(part0)
    part1[...] = jnp.zeros_like(part1)

    pick = tree.astype(jnp.float32)
    side = c.astype(jnp.float32)

    def choose(by, first, second):
        return first * (1.0 - by) + second * by

    def own_step(i):
        phase, source, q, slot = where_is(i, y)
        mine = source == m

        @pl.when(mine)
        def _():
            sib_copy(phase * cuts + q).wait_recv()

        @pl.when(jnp.logical_not(mine))
        def _():
            arrived(phase, slot, q)

        each_hop(i, 0, lambda copy: copy.start())
        a_copy(0, i).wait()

        @pl.when(i + 1 < count)
        def _():
            a_copy(0, i + 1).start()

        multiply(phase, jnp.where(mine, own_slot, slot), q, 0, i, wide == 1)

    def other_step(i):
        phase, _, q, slot = where_is(i, 1 - y)
        arrived(phase, slot, q)
        each_hop(i, 1, lambda copy: copy.start())
        a_copy(1, i).wait()

        @pl.when(i + 1 < count)
        def _():
            a_copy(1, i + 1).start()

        multiply(phase, slot, q, 1, i, True)

    def parents_done():
        link = split(const[0])

        def one(t, carry):
            r = tile_at(t)
            ex_copy(0, t).wait_recv()
            both = -(acc[0, r] + other0[r])
            p0, p1 = both[:, :w], both[:, w:]
            pcol, chosen = choose(side, p0, p1), choose(pick, p0, p1)
            pcol_ref[r] = pcol
            ccol_ref[r] = -dot_split(split(chosen), link)
            part0[:w] += dot_split(split(raw[0, r].T), split(pcol))
            part0[w:] += dot_split(split(chosen.T), split(raw[1, r]))
            return carry

        lax.fori_loop(0, tiles, one, 0)
        sum0.start()

    def diag_done():
        sum0.finish()
        diag = const[1] - whole0[:w]
        diags[0] = diag
        pdiag_ref[0] = diag
        pd_copy().start()

    def step(i, carry):
        if wide == 2:

            @pl.when(i < count)
            def _():
                own_step(i)

            @pl.when(i >= lag)
            def _():
                other_step(i - lag)

        else:
            own_step(i)
        done = i - lag
        pl.when(done == per + per // 6 - 1)(parents_done)
        pl.when(done == per + per // 2 - 1)(sum0.reduce)
        pl.when(done == per + 5 * per // 6 - 1)(diag_done)
        return carry

    lax.fori_loop(0, count + lag, step, 0)

    def children_done(t, carry):
        r = tile_at(t)
        ex_copy(1, t).wait_recv()
        total = choose(side, acc[1, r, :w], acc[1, r, w:]) + other1[r]
        ccol = ccol_ref[r] - total
        ccol_ref[r] = ccol
        part1[...] += dot_split(split(raw[1, r].T), split(ccol))
        return carry

    lax.fori_loop(0, tiles, children_done, 0)
    sum1.start()
    pd_copy().wait()
    first = choose(side, diags[0], diags[1])
    second = choose(side, diags[1], diags[0])
    cross = -(whole0[w:] + dot3(choose(pick, first, second), const[0]))
    cross_ref[0] = cross
    cdiag_ref[0] = const[2] - dot3(const[0].T, cross)
    sum1.reduce()

    @pl.when(m >= half)
    def _():
        def sib_wait(n, carry):
            sib_copy(n).wait_recv()
            return carry

        lax.fori_loop(0, 2 * cuts, sib_wait, 0)

    def drain(i, carry):
        each_hop(i, 0, lambda copy: copy.wait_send())
        if wide == 2:
            each_hop(i, 1, lambda copy: copy.wait_send())
        return carry

    lax.fori_loop(0, count, drain, 0)

    def drain_sib(n, carry):
        sib_copy(n).wait_send()
        return carry

    lax.fori_loop(0, 2 * cuts, drain_sib, 0)

    def drain_ex(t, carry):
        ex_copy(0, t).wait_send()
        ex_copy(1, t).wait_send()
        return carry

    lax.fori_loop(0, tiles, drain_ex, 0)
    sum1.finish()
    cdiag_ref[0] = cdiag_ref[0] - whole1[...]
    sum0.drain()
    sum1.drain()


def per_device(
    wide,
    ancestor_inverse,
    parent_panel,
    child_panel,
    child_link,
    parent_pivot_inv,
    child_pivot_inv,
    parent_blocks,
    child_blocks,
    tree,
):
    rows, w = ancestor_inverse.shape[0], child_link.shape[1]
    line = lax.axis_size("row")
    deep = line // wide
    piece = 256 if rows % 256 == 0 else 128
    tile = piece
    half, cuts, tiles = deep // 2, rows // piece, rows // tile
    count = 2 * half * cuts
    share0, share1 = 2 * w // line, max(8, w // line)
    f32 = jnp.float32
    vmem = pl.BlockSpec(memory_space=pltpu.VMEM)
    dma = pltpu.SemaphoreType.DMA
    flops = 2 * rows * ancestor_inverse.shape[1] * 4 * w * 3
    return pl.pallas_call(
        functools.partial(kernel, (deep, wide, rows, piece, tile, w)),
        out_shape=(
            jax.ShapeDtypeStruct((rows, w), f32),
            jax.ShapeDtypeStruct((1, w, w), f32),
            jax.ShapeDtypeStruct((rows, w), f32),
            jax.ShapeDtypeStruct((1, w, w), f32),
            jax.ShapeDtypeStruct((1, w, w), f32),
        ),
        in_specs=[pl.BlockSpec(memory_space=pl.ANY)] * 9,
        out_specs=(vmem,) * 5,
        scratch_shapes=[
            pltpu.SMEM(tree.shape, jnp.int32),
            pltpu.SMEM(parent_blocks.shape, jnp.int32),
            pltpu.SMEM(child_blocks.shape, jnp.int32),
            pltpu.VMEM((2, half * wide + 1, rows, 2 * w), f32),
            pltpu.VMEM((2, rows, 2 * w), f32),
            pltpu.VMEM((wide, 2, rows, piece), f32),
            pltpu.VMEM((2, piece, 2 * w), jnp.bfloat16),
            pltpu.VMEM((rows, 2 * w), f32),
            pltpu.VMEM((rows, w), f32),
            pltpu.VMEM((2, rows, w), f32),
            pltpu.VMEM((3, w, w), f32),
            pltpu.VMEM((2, w, w), f32),
            pltpu.VMEM((2 * w, w), f32),
            pltpu.VMEM((line, share0, w), f32),
            pltpu.VMEM((2 * w, w), f32),
            pltpu.VMEM((w, w), f32),
            pltpu.VMEM((line, share1, w), f32),
            pltpu.VMEM((w, w), f32),
            dma((8,)),
            dma((2 * cuts,)),
            dma((2 * cuts,)),
            dma((2 * half * wide * cuts,)),
            dma((3, count)),
            dma((2, count)),
            dma((wide, 2)),
            dma((2, tiles)),
            dma((2, tiles)),
            dma((2,)),
            dma((4, line)),
            dma((4, line)),
        ],
        cost_estimate=pl.CostEstimate(
            flops=flops, bytes_accessed=8 * ancestor_inverse.size, transcendentals=0
        ),
        compiler_params=pltpu.CompilerParams(
            collective_id=0, has_side_effects=True, vmem_limit_bytes=56 * 2**20
        ),
    )(
        tree,
        parent_blocks,
        child_blocks,
        parent_panel,
        child_panel,
        ancestor_inverse,
        child_link,
        parent_pivot_inv,
        child_pivot_inv,
    )


def solution(mesh):
    line = list(mesh.devices[0, :, 0])
    places = {getattr(device, "coords", (0, index % 2, 0))[1] for index, device in enumerate(line)}
    wide = 2 if len(places) == 2 else 1
    return jax.shard_map(
        functools.partial(per_device, wide),
        mesh=mesh,
        in_specs=(
            P(("pole", "row"), "col"),
            P(("pole", "row"), "col"),
            P(("pole", "row"), "col"),
            P(("pole", "col"), None, None),
            P(("pole", "col"), None, None),
            P(("pole", "col"), None, None),
            P("pole", None),
            P("pole", None),
            P("pole"),
        ),
        out_specs=(
            P(("pole", "row"), "col"),
            P(("pole", "col"), None, None),
            P(("pole", "row"), "col"),
            P(("pole", "col"), None, None),
            P(("pole", "col"), None, None),
        ),
        check_vma=False,
    )
```

```python
import functools

import jax
import jax.numpy as jnp
from jax import lax
from jax.experimental import pallas as pl
from jax.experimental.pallas import tpu as pltpu
from jax.sharding import PartitionSpec as P

MESH = pl.DeviceIdType.MESH
LAG = 2


def split(value):
    high = value.astype(jnp.bfloat16)
    return high, (value - high.astype(jnp.float32)).astype(jnp.bfloat16)


def dot_split(left, right):
    lh, ll = left
    rh, rl = right
    dot = functools.partial(jnp.dot, preferred_element_type=jnp.float32)
    return dot(lh, rh) + (dot(lh, rl) + dot(ll, rh))


def dot3(left, right):
    return dot_split(split(left), split(right))


class RowSum:
    def __init__(self, line, share, part, terms, whole, sems):
        self.line, self.share, self.part, self.terms, self.whole = line, share, part, terms, whole
        self.sems = sems
        self.owners = part.shape[0] // share
        self.row, self.c = lax.axis_index("row"), lax.axis_index("col")

    def at(self, place):
        return pl.ds(pl.multiple_of(place * self.share, self.share), self.share)

    def copy(self, k, stage, src, dst):
        return pltpu.make_async_remote_copy(
            src_ref=src,
            dst_ref=dst,
            send_sem=self.sems.at[2 * stage, k],
            recv_sem=self.sems.at[2 * stage + 1, k],
            device_id={"row": (self.row + k) % self.line, "col": self.c},
            device_id_type=MESH,
        )

    def scatter(self, k):
        to = (self.row + k) % self.line
        return self.copy(k, 0, self.part.at[self.at(to)], self.terms.at[k])

    def gather(self, k):
        return self.copy(k, 1, self.whole.at[self.at(self.row)], self.whole.at[self.at(self.row)])

    def guard(self, place, act):
        if self.owners == self.line:
            act()
        else:
            pl.when(place < self.owners)(act)

    def loop(self, body):
        def one(k, carry):
            body(k)
            return carry

        lax.fori_loop(1, self.line, one, 0)

    def start(self):
        self.loop(
            lambda k: self.guard((self.row + k) % self.line, lambda: self.scatter(k).start())
        )

    def reduce(self):
        def act():
            def add_term(k, total):
                self.scatter(k).wait_recv()
                return total + self.terms[k]

            mine = self.at(self.row)
            self.whole[mine] = lax.fori_loop(1, self.line, add_term, self.part[mine])
            self.loop(lambda k: self.gather(k).start())

        self.guard(self.row, act)

    def finish(self):
        def one(k):
            origin = (self.row + self.line - k) % self.line
            spot = self.whole.at[self.at(origin)]
            self.guard(origin, lambda: self.copy(k, 1, spot, spot).wait_recv())

        self.loop(one)

    def drain(self):
        self.loop(
            lambda k: self.guard((self.row + k) % self.line, lambda: self.scatter(k).wait_send())
        )
        self.guard(self.row, lambda: self.loop(lambda k: self.gather(k).wait_send()))


def kernel(
    geo, tree_hbm, parents_hbm, kids_hbm, parent_ref, child_ref, a_ref,
    link_ref, pivot_ref, child_pivot_ref,
    pcol_ref, pdiag_ref, ccol_ref, cross_ref, cdiag_ref,
    tree_ref, parents_ref, kids_ref,
    panel, acc, a_buf, halves, other0, other1, raw, const, diags,
    part0, terms0, whole0, part1, terms1, whole1,
    in_sem, sib_send, sib_recv, recv, send, send_more, a_sem, ex_send, ex_recv, pd_sem,
    sems0, sems1,
):
    deep, wide, rows, piece, tile, w = geo
    line = deep * wide
    half, cuts, tiles = deep // 2, rows // piece, rows // tile
    own_slot = half * wide
    per = half * cuts
    count = 2 * per
    lag = LAG if wide == 2 else 0
    row, c = lax.axis_index("row"), lax.axis_index("col")
    z, y = row // wide, row % wide
    m = z + c * (deep - 1 - 2 * z)
    sibling = {"row": row, "col": 1 - c}
    sum0 = RowSum(line, 2 * w // line, part0, terms0, whole0, sems0)
    sum1 = RowSum(line, max(8, w // line), part1, terms1, whole1, sems1)

    def row_at(place, column):
        return (place + c * (deep - 1 - 2 * place)) * wide + column

    def local(source, column):
        return (source + c * (half - 1 - 2 * source)) * wide + column

    def source_of(j):
        left, right = m, half - 1 - m
        both = jnp.minimum(left, right)
        step = (j + 1) // 2
        near = m + jnp.where(j % 2 == 1, step, -step)
        far = jnp.where(left > right, m - (j - both), m + (j - both))
        inside = jnp.where(j <= 2 * both, near, far)
        return jnp.where(m >= half, half - 1 - j, inside)

    def cut(q):
        return pl.ds(pl.multiple_of(q * piece, piece), piece)

    def tile_at(t):
        return pl.ds(pl.multiple_of(t * tile, tile), tile)

    has_right, has_left = m + 1 < deep, m >= 1
    barrier = pltpu.get_barrier_semaphore()
    pl.semaphore_signal(barrier, inc=1, device_id=sibling, device_id_type=MESH)

    def greet(k, carry):
        pl.semaphore_signal(
            barrier, inc=1, device_id={"row": (row + k) % line, "col": c}, device_id_type=MESH
        )
        return carry

    lax.fori_loop(1, line, greet, 0)

    own_lanes = pl.ds(pl.multiple_of(c * w, w), w)

    def sib_copy(n):
        phase, at = n // cuts, cut(n % cuts)
        return pltpu.make_async_remote_copy(
            src_ref=raw.at[phase, at],
            dst_ref=panel.at[phase, own_slot, at, own_lanes],
            send_sem=sib_send.at[n],
            recv_sem=sib_recv.at[n],
            device_id=sibling,
            device_id_type=MESH,
        )

    def pd_copy():
        return pltpu.make_async_remote_copy(
            src_ref=diags.at[0],
            dst_ref=diags.at[1],
            send_sem=pd_sem.at[0],
            recv_sem=pd_sem.at[1],
            device_id=sibling,
            device_id_type=MESH,
        )

    def where_is(i, column):
        phase, rest = i // per, i % per
        source, q = source_of(rest // cuts), rest % cuts
        return phase, source, q, local(source, column)

    def flag(phase, slot, q):
        return (phase * half * wide + slot) * cuts + q

    def a_copy(kind, i):
        column = y if kind == 0 else 1 - y
        _, _, q, slot = where_is(i, column)
        at = pl.ds(pl.multiple_of(slot * rows + q * piece, piece), piece)
        return pltpu.make_async_copy(
            a_ref.at[:, at], a_buf.at[kind, i % 2], a_sem.at[kind, i % 2]
        )

    def hop(way, i, kind):
        column = y if kind == 0 else 1 - y
        phase, source, q, slot = where_is(i, column)
        here = jnp.where(source == m, own_slot, slot) if kind == 0 else slot
        target = (row_at(m + 1, y), row_at(m - 1, y), row_at(m, 1 - y))[way]
        return pltpu.make_async_remote_copy(
            src_ref=panel.at[phase, here, cut(q)],
            dst_ref=panel.at[phase, slot, cut(q)],
            send_sem=(send if kind == 0 else send_more).at[way, i],
            recv_sem=recv.at[flag(phase, slot, q)],
            device_id={"row": target, "col": c},
            device_id_type=MESH,
        )

    def each_hop(i, kind, act):
        _, source, q, _ = where_is(i, y)
        around = q == cuts // 2
        along = around if kind == 1 else True

        @pl.when(has_right & (source <= m) & along)
        def _():
            act(hop(0, i, kind))

        @pl.when(has_left & (source >= m) & along)
        def _():
            act(hop(1, i, kind))

        if wide == 2 and kind == 0:

            @pl.when(jnp.logical_not(around) | (source == m))
            def _():
                act(hop(2, i, kind))

    def arrived(phase, slot, q):
        spot = panel.at[phase, slot, cut(q)]
        pltpu.make_async_remote_copy(
            src_ref=spot,
            dst_ref=spot,
            send_sem=send.at[0, 0],
            recv_sem=recv.at[flag(phase, slot, q)],
            device_id=sibling,
            device_id_type=MESH,
        ).wait_recv()

    def ex_copy(phase, t):
        r = tile_at(t)
        if phase == 0:
            src, dst = acc.at[0, r], other0.at[r]
        else:
            lanes = pl.ds(pl.multiple_of((1 - c) * w, w), w)
            src, dst = acc.at[1, r, lanes], other1.at[r]
        return pltpu.make_async_remote_copy(
            src_ref=src,
            dst_ref=dst,
            send_sem=ex_send.at[phase, t],
            recv_sem=ex_recv.at[phase, t],
            device_id=sibling,
            device_id_type=MESH,
        )

    def multiply(phase, slot, q, kind, i, closes):
        halves[0], halves[1] = split(panel[phase, slot, cut(q)])

        def one(t, carry):
            r = tile_at(t)
            left = split(a_buf[kind, i % 2, r])
            acc[phase, r] += dot_split(left, (halves[0], halves[1]))
            if closes:

                @pl.when(i == per - 1)
                def _():
                    ex_copy(0, t).start()

                @pl.when(i == count - 1)
                def _():
                    ex_copy(1, t).start()

            return carry

        lax.fori_loop(0, tiles, one, 0, unroll=True)

    inputs = (
        (tree_hbm, tree_ref),
        (parents_hbm, parents_ref),
        (kids_hbm, kids_ref),
        (parent_ref, raw.at[0]),
        (child_ref, raw.at[1]),
        (link_ref.at[0], const.at[0]),
        (pivot_ref.at[0], const.at[1]),
        (child_pivot_ref.at[0], const.at[2]),
    )
    loads = [
        pltpu.make_async_copy(src, dst, in_sem.at[n]) for n, (src, dst) in enumerate(inputs)
    ]
    for load in loads:
        load.start()
    a_copy(0, 0).start()
    if wide == 2:
        a_copy(1, 0).start()
    acc[...] = jnp.zeros_like(acc)
    part0[...] = jnp.zeros_like(part0)
    part1[...] = jnp.zeros_like(part1)
    for load in loads:
        load.wait()
    tree = tree_ref[c]
    for b in range(rows // w):
        at = slice(b * w, (b + 1) * w)
        spot = row * (rows // w) + b
        inherited = parents_ref[0, spot] * (1 - tree) + parents_ref[1, spot] * tree
        raw[0, at] = raw[0, at] * parents_ref[c, spot].astype(jnp.float32)
        raw[1, at] = raw[1, at] * (inherited * kids_ref[c, spot]).astype(jnp.float32)
    pl.semaphore_wait(barrier, line)

    def start_sib(n, carry):
        sib_copy(n).start()
        return carry

    lax.fori_loop(0, 2 * cuts, start_sib, 0)
    for core in range(2):

        @pl.when(c == core)
        def _(core=core):
            for phase in range(2):
                panel[phase, own_slot, :, core * w : (core + 1) * w] = raw[phase]


    pick = tree.astype(jnp.float32)
    side = c.astype(jnp.float32)

    def choose(by, first, second):
        return first * (1.0 - by) + second * by

    def own_step(i):
        phase, source, q, slot = where_is(i, y)
        mine = source == m

        @pl.when(mine)
        def _():
            sib_copy(phase * cuts + q).wait_recv()

        @pl.when(jnp.logical_not(mine))
        def _():
            arrived(phase, slot, q)

        each_hop(i, 0, lambda copy: copy.start())
        a_copy(0, i).wait()

        @pl.when(i + 1 < count)
        def _():
            a_copy(0, i + 1).start()

        multiply(phase, jnp.where(mine, own_slot, slot), q, 0, i, wide == 1)

    def other_step(i):
        phase, _, q, slot = where_is(i, 1 - y)
        arrived(phase, slot, q)
        each_hop(i, 1, lambda copy: copy.start())
        a_copy(1, i).wait()

        @pl.when(i + 1 < count)
        def _():
            a_copy(1, i + 1).start()

        multiply(phase, slot, q, 1, i, True)

    def parents_done():
        link = split(const[0])

        def one(t, carry):
            r = tile_at(t)
            ex_copy(0, t).wait_recv()
            both = -(acc[0, r] + other0[r])
            p0, p1 = both[:, :w], both[:, w:]
            pcol, chosen = choose(side, p0, p1), choose(pick, p0, p1)
            pcol_ref[r] = pcol
            ccol_ref[r] = -dot_split(split(chosen), link)
            part0[:w] += dot_split(split(raw[0, r].T), split(pcol))
            part0[w:] += dot_split(split(chosen.T), split(raw[1, r]))
            return carry

        lax.fori_loop(0, tiles, one, 0, unroll=True)
        sum0.start()

    def diag_done():
        sum0.finish()
        diag = const[1] - whole0[:w]
        diags[0] = diag
        pdiag_ref[0] = diag
        pd_copy().start()

    def step(i, carry):
        if wide == 2:

            @pl.when(i < count)
            def _():
                own_step(i)

            @pl.when(i >= lag)
            def _():
                other_step(i - lag)

        else:
            own_step(i)
        done = i - lag
        pl.when(done == per + per // 6 - 1)(parents_done)
        pl.when(done == per + per // 2 - 1)(sum0.reduce)
        pl.when(done == per + 5 * per // 6 - 1)(diag_done)
        return carry

    lax.fori_loop(0, count + lag, step, 0)

    def children_done(t, carry):
        r = tile_at(t)
        ex_copy(1, t).wait_recv()
        total = choose(side, acc[1, r, :w], acc[1, r, w:]) + other1[r]
        ccol = ccol_ref[r] - total
        ccol_ref[r] = ccol
        part1[...] += dot_split(split(raw[1, r].T), split(ccol))
        return carry

    lax.fori_loop(0, tiles, children_done, 0, unroll=True)
    sum1.start()
    pd_copy().wait()
    first = choose(side, diags[0], diags[1])
    second = choose(side, diags[1], diags[0])
    cross = -(whole0[w:] + dot3(choose(pick, first, second), const[0]))
    cross_ref[0] = cross
    cdiag_ref[0] = const[2] - dot3(const[0].T, cross)
    sum1.reduce()

    @pl.when(m >= half)
    def _():
        def sib_wait(n, carry):
            sib_copy(n).wait_recv()
            return carry

        lax.fori_loop(0, 2 * cuts, sib_wait, 0)

    def drain(i, carry):
        each_hop(i, 0, lambda copy: copy.wait_send())
        if wide == 2:
            each_hop(i, 1, lambda copy: copy.wait_send())
        return carry

    lax.fori_loop(0, count, drain, 0)

    def drain_sib(n, carry):
        sib_copy(n).wait_send()
        return carry

    lax.fori_loop(0, 2 * cuts, drain_sib, 0)

    def drain_ex(t, carry):
        ex_copy(0, t).wait_send()
        ex_copy(1, t).wait_send()
        return carry

    lax.fori_loop(0, tiles, drain_ex, 0)
    sum1.finish()
    cdiag_ref[0] = cdiag_ref[0] - whole1[...]
    sum0.drain()
    sum1.drain()


def hand_on(arrays):
    n = len(arrays)

    def body(*refs):
        sources, targets, held, sems = refs[:n], refs[n : 2 * n], refs[2 * n : 3 * n], refs[3 * n]
        for load in range(2):
            pairs = zip(sources, held) if load == 0 else zip(held, targets)
            copies = [
                pltpu.make_async_copy(source, target, sems.at[load, k])
                for k, (source, target) in enumerate(pairs)
            ]
            for copy in copies:
                copy.start()
            for copy in copies:
                copy.wait()

    anywhere = pl.BlockSpec(memory_space=pl.ANY)
    return pl.pallas_call(
        body,
        out_shape=tuple(jax.ShapeDtypeStruct(a.shape, a.dtype) for a in arrays),
        in_specs=[anywhere] * n,
        out_specs=(anywhere,) * n,
        scratch_shapes=[pltpu.VMEM(a.shape, a.dtype) for a in arrays]
        + [pltpu.SemaphoreType.DMA((2, n))],
    )(*arrays)


def per_device(
    wide,
    ancestor_inverse,
    parent_panel,
    child_panel,
    child_link,
    parent_pivot_inv,
    child_pivot_inv,
    parent_blocks,
    child_blocks,
    tree,
):
    rows, w = ancestor_inverse.shape[0], child_link.shape[1]
    line = lax.axis_size("row")
    deep = line // wide
    piece = 256 if rows % 256 == 0 else 128
    tile = piece
    half, cuts, tiles = deep // 2, rows // piece, rows // tile
    count = 2 * half * cuts
    share0, share1 = 2 * w // line, max(8, w // line)
    f32 = jnp.float32
    vmem = pl.BlockSpec(memory_space=pltpu.VMEM)
    dma = pltpu.SemaphoreType.DMA
    flops = 2 * rows * ancestor_inverse.shape[1] * 4 * w * 3
    results = pl.pallas_call(
        functools.partial(kernel, (deep, wide, rows, piece, tile, w)),
        out_shape=(
            jax.ShapeDtypeStruct((rows, w), f32),
            jax.ShapeDtypeStruct((1, w, w), f32),
            jax.ShapeDtypeStruct((rows, w), f32),
            jax.ShapeDtypeStruct((1, w, w), f32),
            jax.ShapeDtypeStruct((1, w, w), f32),
        ),
        in_specs=[pl.BlockSpec(memory_space=pl.ANY)] * 9,
        out_specs=(vmem,) * 5,
        scratch_shapes=[
            pltpu.SMEM(tree.shape, jnp.int32),
            pltpu.SMEM(parent_blocks.shape, jnp.int32),
            pltpu.SMEM(child_blocks.shape, jnp.int32),
            pltpu.VMEM((2, half * wide + 1, rows, 2 * w), f32),
            pltpu.VMEM((2, rows, 2 * w), f32),
            pltpu.VMEM((wide, 2, rows, piece), f32),
            pltpu.VMEM((2, piece, 2 * w), jnp.bfloat16),
            pltpu.VMEM((rows, 2 * w), f32),
            pltpu.VMEM((rows, w), f32),
            pltpu.VMEM((2, rows, w), f32),
            pltpu.VMEM((3, w, w), f32),
            pltpu.VMEM((2, w, w), f32),
            pltpu.VMEM((2 * w, w), f32),
            pltpu.VMEM((line, share0, w), f32),
            pltpu.VMEM((2 * w, w), f32),
            pltpu.VMEM((w, w), f32),
            pltpu.VMEM((line, share1, w), f32),
            pltpu.VMEM((w, w), f32),
            dma((8,)),
            dma((2 * cuts,)),
            dma((2 * cuts,)),
            dma((2 * half * wide * cuts,)),
            dma((3, count)),
            dma((2, count)),
            dma((wide, 2)),
            dma((2, tiles)),
            dma((2, tiles)),
            dma((2,)),
            dma((4, line)),
            dma((4, line)),
        ],
        cost_estimate=pl.CostEstimate(
            flops=flops, bytes_accessed=8 * ancestor_inverse.size, transcendentals=0
        ),
        compiler_params=pltpu.CompilerParams(
            collective_id=0, has_side_effects=True, vmem_limit_bytes=56 * 2**20
        ),
    )(
        tree,
        parent_blocks,
        child_blocks,
        parent_panel,
        child_panel,
        ancestor_inverse,
        child_link,
        parent_pivot_inv,
        child_pivot_inv,
    )
    return hand_on(results)


def solution(mesh):
    line = list(mesh.devices[0, :, 0])
    places = {getattr(device, "coords", (0, index % 2, 0))[1] for index, device in enumerate(line)}
    wide = 2 if len(places) == 2 else 1
    return jax.shard_map(
        functools.partial(per_device, wide),
        mesh=mesh,
        in_specs=(
            P(("pole", "row"), "col"),
            P(("pole", "row"), "col"),
            P(("pole", "row"), "col"),
            P(("pole", "col"), None, None),
            P(("pole", "col"), None, None),
            P(("pole", "col"), None, None),
            P("pole", None),
            P("pole", None),
            P("pole"),
        ),
        out_specs=(
            P(("pole", "row"), "col"),
            P(("pole", "col"), None, None),
            P(("pole", "row"), "col"),
            P(("pole", "col"), None, None),
            P(("pole", "col"), None, None),
        ),
        check_vma=False,
    )
```
